512 devices in a mesh: dp: 32 (over z_lo, y), pipe: 16 (over z_hi, x, core).
Axes of the slice: x: 4, y: 4, z: 16 (z_hi: 2, z_lo: 8; z = z_hi * 8 + z_lo), core: 2. Of those that a mesh axis runs over, the one named last changes fastest.
Arguments:
- tokens: bfloat16 [65536, 4096], P(('dp', 'pipe')), may hold values from -24 to 24
- cotangent: bfloat16 [65536, 4096], P(('dp', 'pipe')), may hold values from -6 to 6
- gate_weight: bfloat16 [256, 4096], P('pipe'), may hold values from -0.09375 to 0.09375
- up_weight: bfloat16 [256, 4096], P('pipe'), may hold values from -0.09375 to 0.09375
- down_weight: bfloat16 [256, 4096], P('pipe'), may hold values from -0.375 to 0.375
Outputs:
- input_grad: bfloat16 [65536, 4096], P(('dp', 'pipe'))
- gate_grad: float32 [256, 4096], P('pipe', 'dp')
- up_grad: float32 [256, 4096], P('pipe', 'dp')
- down_grad: float32 [256, 4096], P('pipe', 'dp')
The draws below stay inside these ranges and needn't reach their ends.
All inputs are finite; a program needn't handle non-finite values.
Results may differ from the reference program's by a relative error of at most 0.005.
Values may be sent and summed in bfloat16 or wider, within the bound.
A program may use at most 64 MiB of HBM per device.

```python
import jax
import jax.numpy as jnp
from jax import lax

D = 4096
TOK_DEV = 128
PANEL = 256
TOKENS = 65536


def strengthened(drawn, stream_key, source, target, shards_of, factor):
    def block_of(axis_at):
        return (jnp.arange(drawn.shape[axis_at]) // (drawn.shape[axis_at] // shards_of)).reshape((-1,) + (1,) * (drawn.ndim - 1 - axis_at))

    first = jax.random.permutation(stream_key, shards_of)[block_of(target)]
    second = (block_of(target) + shards_of // 2) % shards_of
    return jnp.where((block_of(source) == first) | (block_of(source) == second), factor * drawn, drawn)


def steps_of(rng, dims, pieces, smallest, largest):
    def one(axis_at, blocks):
        steps = jax.random.uniform(jax.random.fold_in(jax.random.fold_in(rng, 6), axis_at), (blocks,), jnp.float32, smallest / len(pieces), largest / len(pieces))
        return jnp.repeat(jnp.exp(steps), dims[axis_at] // blocks).reshape((-1,) + (1,) * (len(dims) - axis_at - 1))

    level = one(*pieces[0])
    for cut in pieces[1:]:
        level = level * one(*cut)
    return level


def bell_draw(own_key, extent, scale, reach, shards=(), held_as=jnp.bfloat16):
    array = scale * jax.random.normal(own_key, extent, jnp.float32)
    if shards:
        array = array * steps_of(own_key, extent, shards, -0.22, 0.18)
    return jnp.clip(array, -reach, reach).astype(held_as)


def gaussian_with(stream_key, dims, deviation, reach, pieces, heavy, dtype=jnp.bfloat16):
    array = deviation * jax.random.normal(stream_key, dims, jnp.float32)
    if pieces:
        array = array * steps_of(stream_key, dims, pieces, -0.22, 0.18)
    return jnp.clip(strengthened(array, jax.random.fold_in(stream_key, 3), *heavy), -reach, reach).astype(dtype)


def setup_inputs(seed: int = 0) -> dict:
    arg_keys = jax.random.split(jax.random.key(seed), 6)
    return {
        "tokens": gaussian_with(arg_keys[0], (TOKENS, D), 1.0, 24.0, ((0, 512),), (0, 1, 512, 6.0)),
        "cotangent": bell_draw(arg_keys[1], (TOKENS, D), 1.0, 6.0, ((0, 512),)),
        "gate_weight": bell_draw(arg_keys[2], (PANEL, D), D ** -0.5, 0.09375, ((0, 16),)),
        "up_weight": bell_draw(arg_keys[3], (PANEL, D), D ** -0.5, 0.09375, ((0, 16),)),
        "down_weight": bell_draw(arg_keys[4], (PANEL, D), PANEL ** -0.5, 0.375, ((0, 16),)),
    }


def block_pass(tok_block, cot_block, gate_weight, up_weight, down_weight):
    gate_val = jnp.dot(tok_block, gate_weight.T, preferred_element_type=jnp.float32)
    up_val = jnp.dot(tok_block, up_weight.T, preferred_element_type=jnp.float32)
    sigma = jax.nn.sigmoid(gate_val)
    silu_val = gate_val * sigma
    hidden = (silu_val * up_val).astype(jnp.bfloat16)
    back = jnp.dot(cot_block, down_weight.T, preferred_element_type=jnp.float32)
    up_back = (back * silu_val).astype(jnp.bfloat16)
    gate_back = (back * up_val * sigma * (1.0 + gate_val * (1.0 - sigma))).astype(jnp.bfloat16)
    in_grad = jnp.dot(gate_back, gate_weight, preferred_element_type=jnp.float32)
    in_grad = in_grad + jnp.dot(up_back, up_weight, preferred_element_type=jnp.float32)
    gate_term = jnp.dot(gate_back.T, tok_block, preferred_element_type=jnp.float32).astype(jnp.bfloat16)
    up_term = jnp.dot(up_back.T, tok_block, preferred_element_type=jnp.float32).astype(jnp.bfloat16)
    down_term = jnp.dot(hidden.T, cot_block, preferred_element_type=jnp.float32).astype(jnp.bfloat16)
    stacked = jnp.stack([gate_term, up_term, down_term]).astype(jnp.float32)
    return in_grad.astype(jnp.bfloat16), stacked


def reference(tokens, cotangent, gate_weight, up_weight, down_weight):
    tok_blocks = tokens.reshape(TOKENS // TOK_DEV, TOK_DEV, D)
    cot_blocks = cotangent.reshape(TOKENS // TOK_DEV, TOK_DEV, D)

    def advance(running, pair):
        in_grad, stacked = block_pass(pair[0], pair[1], gate_weight, up_weight, down_weight)
        return running + stacked, in_grad

    initial = jnp.zeros((3, PANEL, D), jnp.float32)
    summed, in_grads = lax.scan(advance, initial, (tok_blocks, cot_blocks))
    grads = summed * (float(TOKENS) ** -0.5)
    return (in_grads.reshape(TOKENS, D), grads[0], grads[1], grads[2])
```

```python
import jax
import jax.numpy as jnp
from jax import lax
from jax.experimental import pallas as pl
from jax.experimental.pallas import tpu as pltpu
from jax.sharding import PartitionSpec as P

F32, BF16 = jnp.float32, jnp.bfloat16
MESH = pl.DeviceIdType.MESH
NX, NY, ZLO, NZ = 4, 4, 8, 16
GATE, UP, DOWN = 0, 1, 2


def panel_kernel(
    scale,
    tok_in, cot_in, wg_in, wu_in, wd_in,
    ig_out, gg_out, ug_out, dg_out,
    tok, cot, w, act, ta, tb, ra, rb, ua, ub, va, vb, zs, zr, ig_send, ig_recv, ig_own,
    load_sem, core_s, core_r, own_xs, own_xr, own_ys, own_yr, hz_s, hz_r, o1_s, o1_r, o2_s, o2_r,
    p1_s, p1_r, p2_s, p2_r, z_s, z_r,
):
    dp, pipe = lax.axis_index("dp"), lax.axis_index("pipe")
    zl, y = dp // NY, dp % NY
    zh, x, c = pipe // 8, (pipe // 2) % NX, pipe % 2
    z = zh * ZLO + zl

    def dev(x_, y_, z_, c_):
        return ((z_ % ZLO) * NY + y_, ((z_ // ZLO) * NX + x_) * 2 + c_)

    def xdev(d):
        return dev((x + d) % NX, y, z, c)

    def ydev(d):
        return dev(x, (y + d) % NY, z, c)

    def zdev(z_):
        return dev(x, y, z_ % NZ, c)

    partner = dev(x, y, z, 1 - c)

    def push(src, dst, ssem, rsem, to):
        pltpu.make_async_remote_copy(src, dst, ssem, rsem, device_id=to, device_id_type=MESH).start()

    def drain(ref, sem):
        pltpu.make_async_copy(ref, ref, sem).wait()

    loads = [
        pltpu.make_async_copy(src, dst, load_sem.at[i])
        for i, (src, dst) in enumerate([
            (wg_in, w.at[GATE, 0:16]), (wu_in, w.at[UP, 0:16]), (wd_in, w.at[DOWN, 0:16]),
            (tok_in, tok.at[0:128]), (cot_in, cot.at[0:128]),
        ])
    ]
    for cp in loads:
        cp.start()

    barrier = pltpu.get_barrier_semaphore()

    def greet(to):
        pl.semaphore_signal(barrier, inc=1, device_id=to, device_id_type=MESH)

    greet(partner)
    for d in range(1, 4):
        greet(xdev(d))
        greet(ydev(d))

    @pl.loop(1, NZ)
    def _(d):
        greet(zdev(z + d))

    pl.semaphore_wait(barrier, 7 + NZ - 1)

    quarter = pl.ds(pl.multiple_of(y * 1024, 1024), 1024)
    eighth0 = pl.ds(pl.multiple_of(y * 512, 512), 512)
    eighth1 = pl.ds(pl.multiple_of(2048 + y * 512, 512), 512)
    pieces = [(GATE, quarter, 1024), (UP, eighth0, 512), (UP, eighth1, 512), (DOWN, quarter, 1024)]

    def from_x(d):
        return pl.ds(16 * (4 - d), 16)

    def other_from_x(d):
        return pl.ds(64 + 16 * (4 - d), 16)

    for cp in loads[:3]:
        cp.wait()
    for t in (GATE, UP):
        for d in (2, 1, 3):
            push(w.at[t, 0:16, quarter], w.at[t, from_x(d), quarter], own_xs.at[t], own_xr.at[t], xdev(d))
    at_edge = (zl == 0) | (zl == ZLO - 1)
    step = jnp.where(zl == 0, NZ - 1, 1)

    @pl.when(at_edge)
    def _():
        for p, (t, cols, _) in enumerate(pieces):
            for dist in (4, 3, 2, 1):
                push(w.at[t, 0:16, cols], w.at[t, 64:80, cols], hz_s.at[p], hz_r.at[p], zdev(z + step * dist))

    for d in (2, 1, 3):
        push(w.at[DOWN, 0:16], w.at[DOWN, from_x(d)], own_xs.at[DOWN], own_xr.at[DOWN], xdev(d))
    loads[3].wait()
    push(tok.at[0:128], tok.at[128:256], core_s.at[0], core_r.at[0], partner)
    loads[4].wait()
    push(cot.at[0:128], cot.at[128:256], core_s.at[1], core_r.at[1], partner)

    for t in (GATE, UP):
        drain(w.at[t, 0:48, 0:1024], own_xr.at[t])
        for d in (2, 1, 3):
            push(w.at[t, 16:64, quarter], w.at[t, 16:64, quarter], own_ys.at[t], own_yr.at[t], ydev(d))

    for p, (t, cols, n) in enumerate(pieces):
        drain(w.at[t, 0:16, 0:n], hz_r.at[p])
        for d in (2, 1, 3):
            if p < 2:
                push(w.at[t, 64:80, cols], w.at[t, other_from_x(d), cols], o1_s.at[p], o1_r.at[p], xdev(d))
            else:
                push(w.at[t, 64:80, cols], w.at[t, 64:80, cols], o1_s.at[p], o1_r.at[p], ydev(d))

    nt = (((1,), (1,)), ((), ()))

    def forward(r):
        rows = slice(64 * r, 64 * r + 64)
        gate = lax.dot_general(w[GATE, rows, :], tok[...], nt, preferred_element_type=F32)
        up = lax.dot_general(w[UP, rows, :], tok[...], nt, preferred_element_type=F32)
        back = lax.dot_general(w[DOWN, rows, :], cot[...], nt, preferred_element_type=F32)
        sigma = jax.nn.sigmoid(gate)
        silu = gate * sigma
        act[r, 0] = (silu * up).astype(BF16)
        act[r, 1] = (back * silu).astype(BF16)
        act[r, 2] = (back * up * sigma * (1.0 + gate * (1.0 - sigma))).astype(BF16)

    def terms(r):
        for first, last, src in ((0, 1, cot), (1, 3, tok)):
            n = last - first
            lhs = act[r, first:last].reshape(64 * n, 256)
            for side in range(2):

                @pl.loop(0, 4)
                def _(q):
                    cols = pl.ds(pl.multiple_of((4 * side + q) * 512, 512), 512)
                    t = jnp.dot(lhs, src[:, cols], preferred_element_type=F32).astype(BF16)
                    for j in range(n):
                        k = 3 * r + first + j
                        for a in range(4):
                            for b in range(4):
                                tile = t[64 * j + 16 * a:64 * j + 16 * a + 16, 128 * b:128 * b + 128]
                                if side == 0:
                                    ta[k, a, b, q] = tile
                                else:
                                    tb[k, b, a, q] = tile

            for j in range(n):
                k = 3 * r + first + j
                for d in (2, 1, 3):
                    push(ta.at[k, d], ra.at[k, d - 1], p1_s.at[k, 0], p1_r.at[k, 0], xdev(d))
                    push(tb.at[k, (y + d) % NY], rb.at[k, d - 1], p1_s.at[k, 1], p1_r.at[k, 1], ydev(d))

    drain(tok.at[0:128], core_r.at[0])
    drain(cot.at[0:128], core_r.at[1])
    drain(w.at[GATE, 0:48, 0:3072], own_yr.at[GATE])
    drain(w.at[UP, 0:48, 0:3072], own_yr.at[UP])
    drain(w.at[DOWN, 0:48], own_xr.at[DOWN])
    forward(0)

    for p, (t, cols, n) in enumerate(pieces):
        drain(w.at[t, 0:48, 0:n], o1_r.at[p])
        row = slice(None) if t == DOWN else slice(2048, 4096)
        for d in (2, 1, 3):
            if p < 2:
                push(w.at[t, 64:128, cols], w.at[t, 64:128, cols], o2_s.at[p], o2_r.at[p], ydev(d))
            else:
                push(w.at[t, 64:80, row], w.at[t, other_from_x(d), row], o2_s.at[p], o2_r.at[p], xdev(d))

    terms(0)

    o2_bytes = [w.at[GATE, 0:64, 0:3072], w.at[UP, 0:64, 0:1536], w.at[UP, 0:48, 0:2048], w.at[DOWN, 0:48]]
    for p in range(4):
        drain(o2_bytes[p], o2_r.at[p])
    forward(1)
    terms(1)

    def both(tokens_at):
        parts = [
            jnp.concatenate([act[0, j, :, tokens_at], act[1, j, :, tokens_at]], axis=0).astype(F32).T
            for j in (2, 1)
        ]
        return jnp.concatenate(parts, axis=1).astype(BF16)

    theirs = both(slice(128, 256))

    @pl.loop(0, 8)
    def _(q):
        cols = pl.ds(pl.multiple_of(q * 512, 512), 512)
        rhs = w[GATE:UP + 1, :, cols].reshape(256, 512)
        ig_send[:, cols] = jnp.dot(theirs, rhs, preferred_element_type=F32).astype(BF16)

    push(ig_send, ig_recv, core_s.at[2], core_r.at[2], partner)

    def input_gradient():
        mine = both(slice(0, 128))
        drain(ig_recv, core_r.at[2])

        @pl.loop(0, 8)
        def _(q):
            cols = pl.ds(pl.multiple_of(q * 512, 512), 512)
            rhs = w[GATE:UP + 1, :, cols].reshape(256, 512)
            total = jnp.dot(mine, rhs, preferred_element_type=F32) + ig_recv[:, cols].astype(F32)
            ig_own[:, cols] = total.astype(BF16)

        pltpu.make_async_copy(ig_own, ig_out, load_sem.at[5]).start()

    def plane_sum(own, got):
        return (own + got[0].astype(F32)) + (got[1].astype(F32) + got[2].astype(F32))

    def first(k):
        drain(ra.at[k], p1_r.at[k, 0])
        ua[k] = plane_sum(ta[k, 0].astype(F32), ra[k]).astype(BF16)
        for d in (2, 1, 3):
            push(ua.at[k, (y + d) % NY], va.at[k, d - 1], p2_s.at[k, 0], p2_r.at[k, 0], ydev(d))
        drain(rb.at[k], p1_r.at[k, 1])
        ub[k] = plane_sum(tb[k, y].astype(F32), rb[k]).astype(BF16)
        for d in (2, 1, 3):
            push(ub.at[k, d], vb.at[k, d - 1], p2_s.at[k, 1], p2_r.at[k, 1], xdev(d))

    def second(k):
        r, j = k // 3, k % 3
        drain(va.at[k], p2_r.at[k, 0])
        zs[k, 0:4] = plane_sum(ua[k, y].astype(F32), va[k]).astype(BF16)
        drain(vb.at[k], p2_r.at[k, 1])
        zs[k, 4:8] = plane_sum(ub[k, 0].astype(F32), vb[k]).astype(BF16)
        if r == 0:
            zr[j, z] = zs[k, zl]
        base = (zh if r == 0 else 1 - zh) * ZLO
        for d in range(1 - r, ZLO):
            to = (zl + d) % ZLO
            push(zs.at[k, to], zr.at[j, z], z_s.at[k], z_r.at[j], zdev(base + to))

    first(0)
    first(1)
    input_gradient()
    for k in range(2, 6):
        second(k - 2)
        first(k)
    second(4)
    second(5)
    for j, out in enumerate((dg_out, ug_out, gg_out)):
        drain(zr.at[j, 0:NZ - 1], z_r.at[j])
        out[...] = jnp.sum(zr[j].astype(F32), axis=0) * scale

    pltpu.make_async_copy(ig_own, ig_out, load_sem.at[5]).wait()
    drain(tok.at[0:128], core_s.at[0])
    drain(cot.at[0:128], core_s.at[1])
    drain(ig_send, core_s.at[2])
    for t in (GATE, UP):
        drain(w.at[t, 0:48, 0:1024], own_xs.at[t])
        drain(w.at[t, 0:48, 0:3072], own_ys.at[t])
    drain(w.at[DOWN, 0:48], own_xs.at[DOWN])

    @pl.when(at_edge)
    def _():
        for p, (t, _, n) in enumerate(pieces):
            drain(w.at[t, 0:64, 0:n], hz_s.at[p])

    for p, (t, _, n) in enumerate(pieces):
        drain(w.at[t, 0:48, 0:n], o1_s.at[p])
        drain(o2_bytes[p], o2_s.at[p])
    for k in range(6):
        drain(ra.at[k], p1_s.at[k, 0])
        drain(rb.at[k], p1_s.at[k, 1])
        drain(va.at[k], p2_s.at[k, 0])
        drain(vb.at[k], p2_s.at[k, 1])
        drain(zs.at[k, 0:7 + k // 3], z_s.at[k])


def per_device(tokens, cotangent, gate_weight, up_weight, down_weight):
    token_total = tokens.shape[0] * lax.axis_size("dp") * lax.axis_size("pipe")
    scale = float(token_total) ** (-0.5)
    anywhere = pl.BlockSpec(memory_space=pl.ANY)
    inside = pl.BlockSpec(memory_space=pltpu.VMEM)
    share = jax.ShapeDtypeStruct((16, 128), F32)

    def body(*refs):
        panel_kernel(scale, *refs)

    def held(*shape):
        return pltpu.VMEM(shape, BF16)

    def sems(*shape):
        return pltpu.SemaphoreType.DMA(shape)

    return pl.pallas_call(
        body,
        out_shape=(jax.ShapeDtypeStruct(tokens.shape, BF16), share, share, share),
        in_specs=[anywhere] * 5,
        out_specs=(anywhere, inside, inside, inside),
        scratch_shapes=[
            held(256, 4096), held(256, 4096), held(3, 128, 4096), held(2, 3, 64, 256),
            held(6, 4, 4, 4, 16, 128), held(6, 4, 4, 4, 16, 128),
            held(6, 3, 4, 4, 16, 128), held(6, 3, 4, 4, 16, 128),
            held(6, 4, 4, 16, 128), held(6, 4, 4, 16, 128),
            held(6, 3, 4, 16, 128), held(6, 3, 4, 16, 128),
            held(6, 8, 16, 128), held(3, 16, 16, 128),
            held(128, 4096), held(128, 4096), held(128, 4096),
            sems(6), sems(3), sems(3), sems(3), sems(3), sems(2), sems(2), sems(4), sems(4),
            sems(4), sems(4), sems(4), sems(4),
            sems(6, 2), sems(6, 2), sems(6, 2), sems(6, 2), sems(6), sems(3),
        ],
        compiler_params=pltpu.CompilerParams(
            collective_id=0, has_side_effects=True, vmem_limit_bytes=48 * 2**20
        ),
    )(tokens, cotangent, gate_weight, up_weight, down_weight)


def solution(mesh):
    in_specs = (
        P(("dp", "pipe"), None),
        P(("dp", "pipe"), None),
        P("pipe", None),
        P("pipe", None),
        P("pipe", None),
    )
    out_specs = (P(("dp", "pipe"), None), P("pipe", "dp"), P("pipe", "dp"), P("pipe", "dp"))
    return jax.shard_map(
        per_device, mesh=mesh, in_specs=in_specs, out_specs=out_specs, check_vma=False
    )
```

```python
import jax
import jax.numpy as jnp
from jax import lax
from jax.experimental import pallas as pl
from jax.experimental.pallas import tpu as pltpu
from jax.sharding import PartitionSpec as P

F32, BF16 = jnp.float32, jnp.bfloat16
MESH = pl.DeviceIdType.MESH
NX, NY, ZLO, NZ = 4, 4, 8, 16
GATE, UP, DOWN = 0, 1, 2
CHUNKS = ((0, 0, 3), (1, 0, 1), (1, 1, 3))


def panel_kernel(
    scale,
    tok_in, cot_in, wg_in, wu_in, wd_in,
    ig_out, grad_out,
    tok, cot, w, act, ig_send, ig_recv, ig_own,
    load_sem, core_s, core_r, own_xs, own_xr, own_ys, own_yr, hz_s, hz_r, o1_s, o1_r, o2_s, o2_r,
    p1_s, p1_r, p2_s, p2_r, z_s, z_r, reach,
    *bufs,
):
    tas, tbs, ras, rbs, uas, ubs, vas, vbs, zss, zrs = (bufs[3 * i:3 * i + 3] for i in range(10))
    dp, pipe = lax.axis_index("dp"), lax.axis_index("pipe")
    zl, y = dp // NY, dp % NY
    zh, x, c = pipe // 8, (pipe // 2) % NX, pipe % 2
    z = zh * ZLO + zl

    def dev(x_, y_, z_, c_):
        return ((z_ % ZLO) * NY + y_, ((z_ // ZLO) * NX + x_) * 2 + c_)

    def xdev(d):
        return dev((x + d) % NX, y, z, c)

    def ydev(d):
        return dev(x, (y + d) % NY, z, c)

    def zdev(z_):
        return dev(x, y, z_ % NZ, c)

    partner = dev(x, y, z, 1 - c)

    def push(src, dst, ssem, rsem, to):
        pltpu.make_async_remote_copy(src, dst, ssem, rsem, device_id=to, device_id_type=MESH).start()

    def drain(ref, sem):
        pltpu.make_async_copy(ref, ref, sem).wait()

    loads = [
        pltpu.make_async_copy(src, dst, load_sem.at[i])
        for i, (src, dst) in enumerate([
            (wg_in, w.at[GATE, 0:16]), (wu_in, w.at[UP, 0:16]), (wd_in, w.at[DOWN, 0:16]),
            (tok_in, tok.at[0:128]), (cot_in, cot.at[0:128]),
        ])
    ]
    for cp in loads:
        cp.start()

    barrier = pltpu.get_barrier_semaphore()

    def greet(to):
        pl.semaphore_signal(barrier, inc=1, device_id=to, device_id_type=MESH)

    greet(partner)
    for d in range(1, 4):
        greet(xdev(d))
        greet(ydev(d))

    for d in range(1, 5):
        greet(zdev(z + d))
        greet(zdev(z + NZ - d))
    pl.semaphore_wait(barrier, 15)
    for d in (4, NZ - 4):
        pl.semaphore_signal(reach, inc=1, device_id=zdev(z + d), device_id_type=MESH)

    quarter = pl.ds(pl.multiple_of(y * 1024, 1024), 1024)
    eighth0 = pl.ds(pl.multiple_of(y * 512, 512), 512)
    eighth1 = pl.ds(pl.multiple_of(2048 + y * 512, 512), 512)
    pieces = [
        (DOWN, quarter, 1024, False), (UP, eighth1, 512, False), (GATE, quarter, 1024, True), (UP, eighth0, 512, True),
    ]

    def from_x(d):
        return pl.ds(16 * (4 - d), 16)

    def other_from_x(d):
        return pl.ds(64 + 16 * (4 - d), 16)

    for cp in loads[:3]:
        cp.wait()
    for t in (GATE, UP):
        for d in (2, 1, 3):
            push(w.at[t, 0:16, quarter], w.at[t, from_x(d), quarter], own_xs.at[t], own_xr.at[t], xdev(d))
    at_edge = (zl == 0) | (zl == ZLO - 1)
    step = jnp.where(zl == 0, NZ - 1, 1)

    @pl.when(at_edge)
    def _():
        for p, (t, cols, _, _) in enumerate(pieces):
            for dist in (4, 3, 2, 1):
                push(w.at[t, 0:16, cols], w.at[t, 64:80, cols], hz_s.at[p], hz_r.at[p], zdev(z + step * dist))

    loads[3].wait()
    push(tok.at[0:128], tok.at[128:256], core_s.at[0], core_r.at[0], partner)
    loads[4].wait()
    push(cot.at[0:128], cot.at[128:256], core_s.at[1], core_r.at[1], partner)
    for d in (2, 1, 3):
        push(w.at[DOWN, 0:16], w.at[DOWN, from_x(d)], own_xs.at[DOWN], own_xr.at[DOWN], xdev(d))

    def own_by_y(t):
        drain(w.at[t, 0:48, 0:1024], own_xr.at[t])
        for d in (2, 1, 3):
            push(w.at[t, 16:64, quarter], w.at[t, 16:64, quarter], own_ys.at[t], own_yr.at[t], ydev(d))

    def other_one(p):
        t, cols, n, by_x = pieces[p]
        drain(w.at[t, 0:16, 0:n], hz_r.at[p])
        for d in (2, 1, 3):
            if by_x:
                push(w.at[t, 64:80, cols], w.at[t, other_from_x(d), cols], o1_s.at[p], o1_r.at[p], xdev(d))
            else:
                push(w.at[t, 64:80, cols], w.at[t, 64:80, cols], o1_s.at[p], o1_r.at[p], ydev(d))

    def other_two(p):
        t, cols, n, by_x = pieces[p]
        drain(w.at[t, 0:48, 0:n], o1_r.at[p])
        row = slice(None) if t == DOWN else slice(2048, 4096)
        for d in (2, 1, 3):
            if by_x:
                push(w.at[t, 64:128, cols], w.at[t, 64:128, cols], o2_s.at[p], o2_r.at[p], ydev(d))
            else:
                push(w.at[t, 64:80, row], w.at[t, other_from_x(d), row], o2_s.at[p], o2_r.at[p], xdev(d))

    own_by_y(GATE)
    other_one(0)
    other_one(1)
    own_by_y(UP)
    other_one(2)
    other_one(3)
    for p in range(4):
        other_two(p)

    nt = (((1,), (1,)), ((), ()))

    def forward(r):
        rows = slice(64 * r, 64 * r + 64)
        gate = lax.dot_general(w[GATE, rows, :], tok[...], nt, preferred_element_type=F32)
        up = lax.dot_general(w[UP, rows, :], tok[...], nt, preferred_element_type=F32)
        back = lax.dot_general(w[DOWN, rows, :], cot[...], nt, preferred_element_type=F32)
        sigma = jax.nn.sigmoid(gate)
        silu = gate * sigma
        act[r, 0] = (silu * up).astype(BF16)
        act[r, 1] = (back * silu).astype(BF16)
        act[r, 2] = (back * up * sigma * (1.0 + gate * (1.0 - sigma))).astype(BF16)

    def terms(k):
        r, start, end = CHUNKS[k]
        for first, last, src in ((0, 1, cot), (1, 3, tok)):
            if not start <= first < end:
                continue
            n = last - first
            lhs = act[r, first:last].reshape(64 * n, 256)
            for side in range(2):

                @pl.loop(0, 4)
                def _(q):
                    cols = pl.ds(pl.multiple_of((4 * side + q) * 512, 512), 512)
                    t = jnp.dot(lhs, src[:, cols], preferred_element_type=F32).astype(BF16)
                    for j in range(n):
                        at = first - start + j
                        for a in range(4):
                            for b in range(4):
                                tile = t[64 * j + 16 * a:64 * j + 16 * a + 16, 128 * b:128 * b + 128]
                                if side == 0:
                                    tas[k][a, b, at, q] = tile
                                else:
                                    tbs[k][b, a, at, q] = tile

                if last == end:
                    for d in (2, 1, 3):
                        if side == 0:
                            push(tas[k].at[d], ras[k].at[d - 1], p1_s.at[k, 0], p1_r.at[k, 0], xdev(d))
                        else:
                            push(tbs[k].at[(y + d) % NY], rbs[k].at[d - 1], p1_s.at[k, 1], p1_r.at[k, 1], ydev(d))

    drain(tok.at[0:128], core_r.at[0])
    drain(cot.at[0:128], core_r.at[1])
    drain(w.at[GATE, 0:48, 0:3072], own_yr.at[GATE])
    drain(w.at[UP, 0:48, 0:3072], own_yr.at[UP])
    drain(w.at[DOWN, 0:48], own_xr.at[DOWN])
    forward(0)
    terms(0)

    o2_bytes = [w.at[DOWN, 0:48], w.at[UP, 0:48, 0:2048], w.at[GATE, 0:64, 0:3072], w.at[UP, 0:64, 0:1536]]
    for p in range(4):
        drain(o2_bytes[p], o2_r.at[p])
    forward(1)
    terms(1)
    terms(2)

    def both(tokens_at):
        parts = [
            jnp.concatenate([act[0, j, :, tokens_at], act[1, j, :, tokens_at]], axis=0).astype(F32).T
            for j in (2, 1)
        ]
        return jnp.concatenate(parts, axis=1).astype(BF16)

    theirs = both(slice(128, 256))

    @pl.loop(0, 8)
    def _(q):
        cols = pl.ds(pl.multiple_of(q * 512, 512), 512)
        rhs = w[GATE:UP + 1, :, cols].reshape(256, 512)
        ig_send[:, cols] = jnp.dot(theirs, rhs, preferred_element_type=F32).astype(BF16)

    push(ig_send, ig_recv, core_s.at[2], core_r.at[2], partner)

    def input_gradient():
        mine = both(slice(0, 128))
        drain(ig_recv, core_r.at[2])

        @pl.loop(0, 8)
        def _(q):
            cols = pl.ds(pl.multiple_of(q * 512, 512), 512)
            rhs = w[GATE:UP + 1, :, cols].reshape(256, 512)
            total = jnp.dot(mine, rhs, preferred_element_type=F32) + ig_recv[:, cols].astype(F32)
            ig_own[:, cols] = total.astype(BF16)

        pltpu.make_async_copy(ig_own, ig_out, load_sem.at[5]).start()

    def plane_sum(own, got):
        return ((own.astype(F32) + got[0].astype(F32)) + (got[1].astype(F32) + got[2].astype(F32))).astype(BF16)

    def first(k):
        ta, tb, ra, rb, ua, ub, va, vb = (b[k] for b in (tas, tbs, ras, rbs, uas, ubs, vas, vbs))
        drain(ra, p1_r.at[k, 0])
        for d in (2, 1, 3, 0):
            to = (y + d) % NY
            ua[to] = plane_sum(ta[0, to], ra[:, to])
            if d:
                push(ua.at[to], va.at[d - 1], p2_s.at[k, 0], p2_r.at[k, 0], ydev(d))
        drain(rb, p1_r.at[k, 1])
        for d in (2, 1, 3, 0):
            ub[d] = plane_sum(tb[y, d], rb[:, d])
            if d:
                push(ub.at[d], vb.at[d - 1], p2_s.at[k, 1], p2_r.at[k, 1], xdev(d))

    def second(k):
        r = CHUNKS[k][0]
        ua, ub, va, vb, zs, zr = (b[k] for b in (uas, ubs, vas, vbs, zss, zrs))
        n = zs.shape[1]
        drain(va, p2_r.at[k, 0])
        for j in range(n):
            zs[0:4, j] = plane_sum(ua[y, j], va[:, j])
        drain(vb, p2_r.at[k, 1])
        for j in range(n):
            zs[4:8, j] = plane_sum(ub[0, j], vb[:, j])
        if r == 0:
            zr[zl] = zs[zl]
        base = (zh if r == 0 else 1 - zh) * ZLO
        for d in ((4, 3, 5, 2, 6, 1, 7) if r == 0 else range(ZLO)):
            to = (zl + d) % ZLO
            push(zs.at[to], zr.at[zl], z_s.at[k], z_r.at[k], zdev(base + to))

    pl.semaphore_wait(reach, 2)
    first(0)
    input_gradient()
    second(0)
    first(1)
    first(2)
    second(1)
    second(2)
    for k, (r, _, _) in enumerate(CHUNKS):
        drain(zrs[k].at[0:7 + r], z_r.at[k])
    for j in range(3):
        late = zrs[1][:, 0] if j == 0 else zrs[2][:, j - 1]
        grad_out[j] = (jnp.sum(zrs[0][:, j].astype(F32), axis=0) + jnp.sum(late.astype(F32), axis=0)) * scale

    pltpu.make_async_copy(ig_own, ig_out, load_sem.at[5]).wait()
    drain(tok.at[0:128], core_s.at[0])
    drain(cot.at[0:128], core_s.at[1])
    drain(ig_send, core_s.at[2])
    for t in (GATE, UP):
        drain(w.at[t, 0:48, 0:1024], own_xs.at[t])
        drain(w.at[t, 0:48, 0:3072], own_ys.at[t])
    drain(w.at[DOWN, 0:48], own_xs.at[DOWN])

    @pl.when(at_edge)
    def _():
        for p, (t, _, n, _) in enumerate(pieces):
            drain(w.at[t, 0:64, 0:n], hz_s.at[p])

    for p, (t, _, n, _) in enumerate(pieces):
        drain(w.at[t, 0:48, 0:n], o1_s.at[p])
        drain(o2_bytes[p], o2_s.at[p])
    for k, (r, _, _) in enumerate(CHUNKS):
        drain(ras[k], p1_s.at[k, 0])
        drain(rbs[k], p1_s.at[k, 1])
        drain(vas[k], p2_s.at[k, 0])
        drain(vbs[k], p2_s.at[k, 1])
        drain(zss[k].at[0:7 + r], z_s.at[k])


def finish_kernel(ig, grads, ig_out, gate_out, up_out, down_out, sem):
    pairs = [(ig.at[pl.ds(32 * i, 32)], ig_out.at[pl.ds(32 * i, 32)]) for i in range(4)]
    pairs += [(grads.at[2], gate_out), (grads.at[1], up_out), (grads.at[0], down_out)]
    copies = [pltpu.make_async_copy(src, dst, sem.at[i]) for i, (src, dst) in enumerate(pairs)]
    for cp in copies:
        cp.start()
    for cp in copies:
        cp.wait()


def per_device(tokens, cotangent, gate_weight, up_weight, down_weight):
    token_total = tokens.shape[0] * lax.axis_size("dp") * lax.axis_size("pipe")
    scale = float(token_total) ** (-0.5)
    anywhere = pl.BlockSpec(memory_space=pl.ANY)
    inside = pl.BlockSpec(memory_space=pltpu.VMEM)
    share = jax.ShapeDtypeStruct((16, 128), F32)

    def body(*refs):
        panel_kernel(scale, *refs)

    def held(*shape):
        return pltpu.VMEM(shape, BF16)

    def sems(*shape):
        return pltpu.SemaphoreType.DMA(shape)

    def chunked(*dims):
        shapes = [[last - first if d is None else d for d in dims] for _, first, last in CHUNKS]
        return [held(*dims_, 16, 128) for dims_ in shapes]

    ig, grads = pl.pallas_call(
        body,
        out_shape=(jax.ShapeDtypeStruct(tokens.shape, BF16), jax.ShapeDtypeStruct((3, 16, 128), F32)),
        in_specs=[anywhere] * 5,
        out_specs=(anywhere, inside),
        scratch_shapes=[
            held(256, 4096), held(256, 4096), held(3, 128, 4096), held(2, 3, 64, 256),
            held(128, 4096), held(128, 4096), held(128, 4096),
            sems(6), sems(3), sems(3), sems(3), sems(3), sems(2), sems(2), sems(4), sems(4),
            sems(4), sems(4), sems(4), sems(4),
            sems(3, 2), sems(3, 2), sems(3, 2), sems(3, 2), sems(3), sems(3), pltpu.SemaphoreType.REGULAR,
            *chunked(4, 4, None, 4), *chunked(4, 4, None, 4), *chunked(3, 4, None, 4), *chunked(3, 4, None, 4),
            *chunked(4, None, 4), *chunked(4, None, 4), *chunked(3, None, 4), *chunked(3, None, 4),
            *chunked(8, None), *chunked(8, None),
        ],
        compiler_params=pltpu.CompilerParams(
            collective_id=0, has_side_effects=True, vmem_limit_bytes=60 * 2**20
        ),
    )(tokens, cotangent, gate_weight, up_weight, down_weight)
    return pl.pallas_call(
        finish_kernel,
        out_shape=(jax.ShapeDtypeStruct(tokens.shape, BF16), share, share, share),
        in_specs=[inside] * 2,
        out_specs=[anywhere] * 4,
        scratch_shapes=[sems(7)],
    )(ig, grads)


def solution(mesh):
    in_specs = (
        P(("dp", "pipe"), None),
        P(("dp", "pipe"), None),
        P("pipe", None),
        P("pipe", None),
        P("pipe", None),
    )
    out_specs = (P(("dp", "pipe"), None), P("pipe", "dp"), P("pipe", "dp"), P("pipe", "dp"))
    return jax.shard_map(
        per_device, mesh=mesh, in_specs=in_specs, out_specs=out_specs, check_vma=False
    )
```

```python
import jax
import jax.numpy as jnp
from jax import lax
from jax.experimental import pallas as pl
from jax.experimental.pallas import tpu as pltpu
from jax.sharding import PartitionSpec as P

F32, BF16 = jnp.float32, jnp.bfloat16
MESH = pl.DeviceIdType.MESH
NX, NY, ZLO, NZ = 4, 4, 8, 16
GATE, UP, DOWN = 0, 1, 2
CHUNKS = ((0, 0, 3), (1, 0, 1), (1, 1, 3))


def panel_kernel(
    scale,
    tok_in, cot_in, wg_in, wu_in, wd_in,
    ig_out, grad_out,
    tok, cot, w, act, ig_send, ig_recv, ig_own,
    load_sem, core_s, core_r, own_xs, own_xr, own_ys, own_yr, hz_s, hz_r, o1_s, o1_r, o2_s, o2_r,
    p1_s, p1_r, p2_s, p2_r, z_s, z_r, reach,
    *bufs,
):
    tas, tbs, ras, rbs, uas, ubs, vas, vbs, zss, zrs = (bufs[3 * i:3 * i + 3] for i in range(10))
    dp, pipe = lax.axis_index("dp"), lax.axis_index("pipe")
    zl, y = dp // NY, dp % NY
    zh, x, c = pipe // 8, (pipe // 2) % NX, pipe % 2
    z = zh * ZLO + zl

    def dev(x_, y_, z_, c_):
        return ((z_ % ZLO) * NY + y_, ((z_ // ZLO) * NX + x_) * 2 + c_)

    def xdev(d):
        return dev((x + d) % NX, y, z, c)

    def ydev(d):
        return dev(x, (y + d) % NY, z, c)

    def zdev(z_):
        return dev(x, y, z_ % NZ, c)

    partner = dev(x, y, z, 1 - c)

    def push(src, dst, ssem, rsem, to):
        pltpu.make_async_remote_copy(src, dst, ssem, rsem, device_id=to, device_id_type=MESH).start()

    def drain(ref, sem):
        pltpu.make_async_copy(ref, ref, sem).wait()

    loads = [
        pltpu.make_async_copy(src, dst, load_sem.at[i])
        for i, (src, dst) in enumerate([
            (wg_in, w.at[GATE, 0:16]), (wu_in, w.at[UP, 0:16]), (wd_in, w.at[DOWN, 0:16]),
            (tok_in, tok.at[0:128]), (cot_in, cot.at[0:128]),
        ])
    ]
    for cp in loads:
        cp.start()

    barrier = pltpu.get_barrier_semaphore()

    def greet(to):
        pl.semaphore_signal(barrier, inc=1, device_id=to, device_id_type=MESH)

    greet(partner)
    for d in range(1, 4):
        greet(xdev(d))
        greet(ydev(d))

    for d in range(1, 5):
        greet(zdev(z + d))
        greet(zdev(z + NZ - d))
    pl.semaphore_wait(barrier, 15)
    for d in (4, NZ - 4):
        pl.semaphore_signal(reach, inc=1, device_id=zdev(z + d), device_id_type=MESH)

    quarter = pl.ds(pl.multiple_of(y * 1024, 1024), 1024)
    eighth0 = pl.ds(pl.multiple_of(y * 512, 512), 512)
    eighth1 = pl.ds(pl.multiple_of(2048 + y * 512, 512), 512)
    pieces = [
        (DOWN, quarter, 1024, False), (UP, eighth1, 512, False), (GATE, quarter, 1024, True), (UP, eighth0, 512, True),
    ]

    def from_x(d):
        return pl.ds(16 * (4 - d), 16)

    def other_from_x(d):
        return pl.ds(64 + 16 * (4 - d), 16)

    for cp in loads[:3]:
        cp.wait()
    for t in (GATE, UP):
        for d in (2, 1, 3):
            push(w.at[t, 0:16, quarter], w.at[t, from_x(d), quarter], own_xs.at[t], own_xr.at[t], xdev(d))
    at_edge = (zl == 0) | (zl == ZLO - 1)
    step = jnp.where(zl == 0, NZ - 1, 1)

    @pl.when(at_edge)
    def _():
        for p, (t, cols, _, _) in enumerate(pieces):
            for dist in (4, 3, 2, 1):
                push(w.at[t, 0:16, cols], w.at[t, 64:80, cols], hz_s.at[p], hz_r.at[p], zdev(z + step * dist))

    for d in (2, 1, 3):
        push(w.at[DOWN, 0:16], w.at[DOWN, from_x(d)], own_xs.at[DOWN], own_xr.at[DOWN], xdev(d))

    def own_by_y(t):
        drain(w.at[t, 0:48, 0:1024], own_xr.at[t])
        for d in (2, 1, 3):
            push(w.at[t, 16:64, quarter], w.at[t, 16:64, quarter], own_ys.at[t], own_yr.at[t], ydev(d))

    def other_one(p):
        t, cols, n, by_x = pieces[p]
        drain(w.at[t, 0:16, 0:n], hz_r.at[p])
        for d in (2, 1, 3):
            if by_x:
                push(w.at[t, 64:80, cols], w.at[t, other_from_x(d), cols], o1_s.at[p], o1_r.at[p], xdev(d))
            else:
                push(w.at[t, 64:80, cols], w.at[t, 64:80, cols], o1_s.at[p], o1_r.at[p], ydev(d))

    def other_two(p):
        t, cols, n, by_x = pieces[p]
        drain(w.at[t, 0:48, 0:n], o1_r.at[p])
        row = slice(None) if t == DOWN else slice(2048, 4096)
        for d in (2, 1, 3):
            if by_x:
                push(w.at[t, 64:128, cols], w.at[t, 64:128, cols], o2_s.at[p], o2_r.at[p], ydev(d))
            else:
                push(w.at[t, 64:80, row], w.at[t, other_from_x(d), row], o2_s.at[p], o2_r.at[p], xdev(d))

    own_by_y(GATE)
    loads[3].wait()
    push(tok.at[0:128], tok.at[128:256], core_s.at[0], core_r.at[0], partner)
    loads[4].wait()
    push(cot.at[0:128], cot.at[128:256], core_s.at[1], core_r.at[1], partner)
    other_one(0)
    other_one(1)
    own_by_y(UP)
    other_one(2)
    other_one(3)
    for p in range(4):
        other_two(p)

    nt = (((1,), (1,)), ((), ()))

    def forward(r):
        rows = slice(64 * r, 64 * r + 64)
        gate = lax.dot_general(w[GATE, rows, :], tok[...], nt, preferred_element_type=F32)
        up = lax.dot_general(w[UP, rows, :], tok[...], nt, preferred_element_type=F32)
        back = lax.dot_general(w[DOWN, rows, :], cot[...], nt, preferred_element_type=F32)
        sigma = jax.nn.sigmoid(gate)
        silu = gate * sigma
        act[r, 0] = (silu * up).astype(BF16)
        act[r, 1] = (back * silu).astype(BF16)
        act[r, 2] = (back * up * sigma * (1.0 + gate * (1.0 - sigma))).astype(BF16)

    def terms(k):
        r, start, end = CHUNKS[k]
        for first, last, src in ((0, 1, cot), (1, 3, tok)):
            if not start <= first < end:
                continue
            n = last - first
            lhs = act[r, first:last].reshape(64 * n, 256)
            for side in range(2):

                @pl.loop(0, 4)
                def _(q):
                    cols = pl.ds(pl.multiple_of((4 * side + q) * 512, 512), 512)
                    t = jnp.dot(lhs, src[:, cols], preferred_element_type=F32).astype(BF16)
                    for j in range(n):
                        at = first - start + j
                        for a in range(4):
                            for b in range(4):
                                tile = t[64 * j + 16 * a:64 * j + 16 * a + 16, 128 * b:128 * b + 128]
                                if side == 0:
                                    tas[k][a, b, at, q] = tile
                                else:
                                    tbs[k][b, a, at, q] = tile

                if last == end:
                    for d in (2, 1, 3):
                        if side == 0:
                            push(tas[k].at[d], ras[k].at[d - 1], p1_s.at[k, 0], p1_r.at[k, 0], xdev(d))
                        else:
                            push(tbs[k].at[(y + d) % NY], rbs[k].at[d - 1], p1_s.at[k, 1], p1_r.at[k, 1], ydev(d))

    drain(tok.at[0:128], core_r.at[0])
    drain(cot.at[0:128], core_r.at[1])
    drain(w.at[GATE, 0:48, 0:3072], own_yr.at[GATE])
    drain(w.at[UP, 0:48, 0:3072], own_yr.at[UP])
    drain(w.at[DOWN, 0:48], own_xr.at[DOWN])
    forward(0)
    terms(0)

    o2_bytes = [w.at[DOWN, 0:48], w.at[UP, 0:48, 0:2048], w.at[GATE, 0:64, 0:3072], w.at[UP, 0:64, 0:1536]]
    for p in range(4):
        drain(o2_bytes[p], o2_r.at[p])
    forward(1)
    terms(1)
    terms(2)

    def both(tokens_at):
        parts = [
            jnp.concatenate([act[0, j, :, tokens_at], act[1, j, :, tokens_at]], axis=0).astype(F32).T
            for j in (2, 1)
        ]
        return jnp.concatenate(parts, axis=1).astype(BF16)

    theirs = both(slice(128, 256))

    @pl.loop(0, 8)
    def _(q):
        cols = pl.ds(pl.multiple_of(q * 512, 512), 512)
        rhs = w[GATE:UP + 1, :, cols].reshape(256, 512)
        ig_send[:, cols] = jnp.dot(theirs, rhs, preferred_element_type=F32).astype(BF16)

    push(ig_send, ig_recv, core_s.at[2], core_r.at[2], partner)

    def input_gradient():
        mine = both(slice(0, 128))
        drain(ig_recv, core_r.at[2])

        @pl.loop(0, 8)
        def _(q):
            cols = pl.ds(pl.multiple_of(q * 512, 512), 512)
            rhs = w[GATE:UP + 1, :, cols].reshape(256, 512)
            total = jnp.dot(mine, rhs, preferred_element_type=F32) + ig_recv[:, cols].astype(F32)
            ig_own[:, cols] = total.astype(BF16)

        pltpu.make_async_copy(ig_own, ig_out, load_sem.at[5]).start()

    def plane_sum(own, got):
        return ((own.astype(F32) + got[0].astype(F32)) + (got[1].astype(F32) + got[2].astype(F32))).astype(BF16)

    def first(k):
        ta, tb, ra, rb, ua, ub, va, vb = (b[k] for b in (tas, tbs, ras, rbs, uas, ubs, vas, vbs))
        drain(ra, p1_r.at[k, 0])
        for d in (2, 1, 3, 0):
            to = (y + d) % NY
            ua[to] = plane_sum(ta[0, to], ra[:, to])
            if d:
                push(ua.at[to], va.at[d - 1], p2_s.at[k, 0], p2_r.at[k, 0], ydev(d))
        drain(rb, p1_r.at[k, 1])
        for d in (2, 1, 3, 0):
            ub[d] = plane_sum(tb[y, d], rb[:, d])
            if d:
                push(ub.at[d], vb.at[d - 1], p2_s.at[k, 1], p2_r.at[k, 1], xdev(d))

    def second(k):
        r = CHUNKS[k][0]
        ua, ub, va, vb, zs, zr = (b[k] for b in (uas, ubs, vas, vbs, zss, zrs))
        n = zs.shape[1]
        drain(va, p2_r.at[k, 0])
        for j in range(n):
            zs[0:4, j] = plane_sum(ua[y, j], va[:, j])
        drain(vb, p2_r.at[k, 1])
        for j in range(n):
            zs[4:8, j] = plane_sum(ub[0, j], vb[:, j])
        if r == 0:
            zr[zl] = zs[zl]
        base = (zh if r == 0 else 1 - zh) * ZLO
        for d in ((4, 3, 5, 2, 6, 1, 7) if r == 0 else range(ZLO)):
            to = (zl + d) % ZLO
            push(zs.at[to], zr.at[zl], z_s.at[k], z_r.at[k], zdev(base + to))

    pl.semaphore_wait(reach, 2)
    first(0)
    first(1)
    input_gradient()
    first(2)
    second(0)
    second(1)
    second(2)
    for k, (r, _, _) in enumerate(CHUNKS):
        drain(zrs[k].at[0:7 + r], z_r.at[k])
    for j in range(3):
        late = zrs[1][:, 0] if j == 0 else zrs[2][:, j - 1]
        grad_out[j] = (jnp.sum(zrs[0][:, j].astype(F32), axis=0) + jnp.sum(late.astype(F32), axis=0)) * scale

    pltpu.make_async_copy(ig_own, ig_out, load_sem.at[5]).wait()
    drain(tok.at[0:128], core_s.at[0])
    drain(cot.at[0:128], core_s.at[1])
    drain(ig_send, core_s.at[2])
    for t in (GATE, UP):
        drain(w.at[t, 0:48, 0:1024], own_xs.at[t])
        drain(w.at[t, 0:48, 0:3072], own_ys.at[t])
    drain(w.at[DOWN, 0:48], own_xs.at[DOWN])

    @pl.when(at_edge)
    def _():
        for p, (t, _, n, _) in enumerate(pieces):
            drain(w.at[t, 0:64, 0:n], hz_s.at[p])

    for p, (t, _, n, _) in enumerate(pieces):
        drain(w.at[t, 0:48, 0:n], o1_s.at[p])
        drain(o2_bytes[p], o2_s.at[p])
    for k, (r, _, _) in enumerate(CHUNKS):
        drain(ras[k], p1_s.at[k, 0])
        drain(rbs[k], p1_s.at[k, 1])
        drain(vas[k], p2_s.at[k, 0])
        drain(vbs[k], p2_s.at[k, 1])
        drain(zss[k].at[0:7 + r], z_s.at[k])


def finish_kernel(ig, grads, ig_out, gate_out, up_out, down_out, sem):
    pairs = [(ig.at[pl.ds(32 * i, 32)], ig_out.at[pl.ds(32 * i, 32)]) for i in range(4)]
    pairs += [(grads.at[2], gate_out), (grads.at[1], up_out), (grads.at[0], down_out)]
    copies = [pltpu.make_async_copy(src, dst, sem.at[i]) for i, (src, dst) in enumerate(pairs)]
    for cp in copies:
        cp.start()
    for cp in copies:
        cp.wait()


def per_device(tokens, cotangent, gate_weight, up_weight, down_weight):
    token_total = tokens.shape[0] * lax.axis_size("dp") * lax.axis_size("pipe")
    scale = float(token_total) ** (-0.5)
    anywhere = pl.BlockSpec(memory_space=pl.ANY)
    inside = pl.BlockSpec(memory_space=pltpu.VMEM)
    share = jax.ShapeDtypeStruct((16, 128), F32)

    def body(*refs):
        panel_kernel(scale, *refs)

    def held(*shape):
        return pltpu.VMEM(shape, BF16)

    def sems(*shape):
        return pltpu.SemaphoreType.DMA(shape)

    def chunked(*dims):
        shapes = [[last - first if d is None else d for d in dims] for _, first, last in CHUNKS]
        return [held(*dims_, 16, 128) for dims_ in shapes]

    ig, grads = pl.pallas_call(
        body,
        out_shape=(jax.ShapeDtypeStruct(tokens.shape, BF16), jax.ShapeDtypeStruct((3, 16, 128), F32)),
        in_specs=[anywhere] * 5,
        out_specs=(anywhere, inside),
        scratch_shapes=[
            held(256, 4096), held(256, 4096), held(3, 128, 4096), held(2, 3, 64, 256),
            held(128, 4096), held(128, 4096), held(128, 4096),
            sems(6), sems(3), sems(3), sems(3), sems(3), sems(2), sems(2), sems(4), sems(4),
            sems(4), sems(4), sems(4), sems(4),
            sems(3, 2), sems(3, 2), sems(3, 2), sems(3, 2), sems(3), sems(3), pltpu.SemaphoreType.REGULAR,
            *chunked(4, 4, None, 4), *chunked(4, 4, None, 4), *chunked(3, 4, None, 4), *chunked(3, 4, None, 4),
            *chunked(4, None, 4), *chunked(4, None, 4), *chunked(3, None, 4), *chunked(3, None, 4),
            *chunked(8, None), *chunked(8, None),
        ],
        compiler_params=pltpu.CompilerParams(
            collective_id=0, has_side_effects=True, vmem_limit_bytes=60 * 2**20
        ),
    )(tokens, cotangent, gate_weight, up_weight, down_weight)
    return pl.pallas_call(
        finish_kernel,
        out_shape=(jax.ShapeDtypeStruct(tokens.shape, BF16), share, share, share),
        in_specs=[inside] * 2,
        out_specs=[anywhere] * 4,
        scratch_shapes=[sems(7)],
    )(ig, grads)


def solution(mesh):
    in_specs = (
        P(("dp", "pipe"), None),
        P(("dp", "pipe"), None),
        P("pipe", None),
        P("pipe", None),
        P("pipe", None),
    )
    out_specs = (P(("dp", "pipe"), None), P("pipe", "dp"), P("pipe", "dp"), P("pipe", "dp"))
    return jax.shard_map(
        per_device, mesh=mesh, in_specs=in_specs, out_specs=out_specs, check_vma=False
    )
```

```python
import jax
import jax.numpy as jnp
from jax import lax
from jax.experimental import pallas as pl
from jax.experimental.pallas import tpu as pltpu
from jax.sharding import PartitionSpec as P

F32, BF16 = jnp.float32, jnp.bfloat16
MESH = pl.DeviceIdType.MESH
NX, NY, ZLO, NZ = 4, 4, 8, 16
GATE, UP, DOWN = 0, 1, 2
CHUNKS = ((0, 0, 3), (1, 0, 1), (1, 1, 3))


def panel_kernel(
    scale,
    tok_in, cot_in, wg_in, wu_in, wd_in,
    ig_out, grad_out,
    tok, cot, w, act, ig_send, ig_recv, ig_own,
    load_sem, core_s, core_r, own_xs, own_xr, own_ys, own_yr, hz_s, hz_r, o1_s, o1_r, o2_s, o2_r,
    p1_s, p1_r, p2_s, p2_r, z_s, z_r, reach,
    *bufs,
):
    tas, tbs, ras, rbs, uas, ubs, vas, vbs, zss, zrs = (bufs[3 * i:3 * i + 3] for i in range(10))
    dp, pipe = lax.axis_index("dp"), lax.axis_index("pipe")
    zl, y = dp // NY, dp % NY
    zh, x, c = pipe // 8, (pipe // 2) % NX, pipe % 2
    z = zh * ZLO + zl

    def dev(x_, y_, z_, c_):
        return ((z_ % ZLO) * NY + y_, ((z_ // ZLO) * NX + x_) * 2 + c_)

    def xdev(d):
        return dev((x + d) % NX, y, z, c)

    def ydev(d):
        return dev(x, (y + d) % NY, z, c)

    def zdev(z_):
        return dev(x, y, z_ % NZ, c)

    partner = dev(x, y, z, 1 - c)

    def push(src, dst, ssem, rsem, to):
        pltpu.make_async_remote_copy(src, dst, ssem, rsem, device_id=to, device_id_type=MESH).start()

    def drain(ref, sem):
        pltpu.make_async_copy(ref, ref, sem).wait()

    loads = [
        pltpu.make_async_copy(src, dst, load_sem.at[i])
        for i, (src, dst) in enumerate([
            (wg_in, w.at[GATE, 0:16]), (wu_in, w.at[UP, 0:16]), (wd_in, w.at[DOWN, 0:16]),
            (tok_in, tok.at[0:128]), (cot_in, cot.at[0:128]),
        ])
    ]
    for cp in loads:
        cp.start()

    barrier = pltpu.get_barrier_semaphore()

    def greet(to):
        pl.semaphore_signal(barrier, inc=1, device_id=to, device_id_type=MESH)

    greet(partner)
    for d in range(1, 4):
        greet(xdev(d))
        greet(ydev(d))

    for d in range(1, 5):
        greet(zdev(z + d))
        greet(zdev(z + NZ - d))
    pl.semaphore_wait(barrier, 15)
    for d in (4, NZ - 4):
        pl.semaphore_signal(reach, inc=1, device_id=zdev(z + d), device_id_type=MESH)

    quarter = pl.ds(pl.multiple_of(y * 1024, 1024), 1024)
    eighth0 = pl.ds(pl.multiple_of(y * 512, 512), 512)
    eighth1 = pl.ds(pl.multiple_of(2048 + y * 512, 512), 512)
    pieces = [
        (DOWN, quarter, 1024, False), (UP, eighth1, 512, False), (GATE, quarter, 1024, True), (UP, eighth0, 512, True),
    ]

    def from_x(d):
        return pl.ds(16 * (4 - d), 16)

    def other_from_x(d):
        return pl.ds(64 + 16 * (4 - d), 16)

    for cp in loads[:3]:
        cp.wait()
    for t in (GATE, UP):
        for d in (2, 1, 3):
            push(w.at[t, 0:16, quarter], w.at[t, from_x(d), quarter], own_xs.at[t], own_xr.at[t], xdev(d))
    at_edge = (zl == 0) | (zl == ZLO - 1)
    step = jnp.where(zl == 0, NZ - 1, 1)

    @pl.when(at_edge)
    def _():
        for p, (t, cols, _, _) in enumerate(pieces):
            for dist in (4, 3, 2, 1):
                push(w.at[t, 0:16, cols], w.at[t, 64:80, cols], hz_s.at[p], hz_r.at[p], zdev(z + step * dist))

    for d in (2, 1, 3):
        push(w.at[DOWN, 0:16], w.at[DOWN, from_x(d)], own_xs.at[DOWN], own_xr.at[DOWN], xdev(d))

    def own_by_y(t):
        drain(w.at[t, 0:48, 0:1024], own_xr.at[t])
        for d in (2, 1, 3):
            push(w.at[t, 16:64, quarter], w.at[t, 16:64, quarter], own_ys.at[t], own_yr.at[t], ydev(d))

    def other_one(p):
        t, cols, n, by_x = pieces[p]
        drain(w.at[t, 0:16, 0:n], hz_r.at[p])
        for d in (2, 1, 3):
            if by_x:
                push(w.at[t, 64:80, cols], w.at[t, other_from_x(d), cols], o1_s.at[p], o1_r.at[p], xdev(d))
            else:
                push(w.at[t, 64:80, cols], w.at[t, 64:80, cols], o1_s.at[p], o1_r.at[p], ydev(d))

    def other_two(p):
        t, cols, n, by_x = pieces[p]
        drain(w.at[t, 0:48, 0:n], o1_r.at[p])
        row = slice(None) if t == DOWN else slice(2048, 4096)
        for d in (2, 1, 3):
            if by_x:
                push(w.at[t, 64:128, cols], w.at[t, 64:128, cols], o2_s.at[p], o2_r.at[p], ydev(d))
            else:
                push(w.at[t, 64:80, row], w.at[t, other_from_x(d), row], o2_s.at[p], o2_r.at[p], xdev(d))

    own_by_y(GATE)
    loads[3].wait()
    push(tok.at[0:128], tok.at[128:256], core_s.at[0], core_r.at[0], partner)
    loads[4].wait()
    push(cot.at[0:128], cot.at[128:256], core_s.at[1], core_r.at[1], partner)
    other_one(0)
    other_one(1)
    own_by_y(UP)
    other_one(2)
    other_one(3)
    for p in range(4):
        other_two(p)

    nt = (((1,), (1,)), ((), ()))

    def forward(r, arrive):
        rows = slice(64 * r, 64 * r + 64)
        arrive(0)
        back = lax.dot_general(w[DOWN, rows, :], cot[...], nt, preferred_element_type=F32)
        arrive(1)
        up = lax.dot_general(w[UP, rows, 2048:4096], tok[:, 2048:4096], nt, preferred_element_type=F32)
        arrive(2)
        gate = lax.dot_general(w[GATE, rows, :], tok[...], nt, preferred_element_type=F32)
        arrive(3)
        up = up + lax.dot_general(w[UP, rows, 0:2048], tok[:, 0:2048], nt, preferred_element_type=F32)
        sigma = jax.nn.sigmoid(gate)
        silu = gate * sigma
        act[r, 0] = (silu * up).astype(BF16)
        act[r, 1] = (back * silu).astype(BF16)
        act[r, 2] = (back * up * sigma * (1.0 + gate * (1.0 - sigma))).astype(BF16)

    def terms(k):
        r, start, end = CHUNKS[k]
        for first, last, src in ((0, 1, cot), (1, 3, tok)):
            if not start <= first < end:
                continue
            n = last - first
            lhs = act[r, first:last].reshape(64 * n, 256)
            for side in range(2):

                @pl.loop(0, 4)
                def _(q):
                    cols = pl.ds(pl.multiple_of((4 * side + q) * 512, 512), 512)
                    t = jnp.dot(lhs, src[:, cols], preferred_element_type=F32).astype(BF16)
                    for j in range(n):
                        at = first - start + j
                        for a in range(4):
                            for b in range(4):
                                tile = t[64 * j + 16 * a:64 * j + 16 * a + 16, 128 * b:128 * b + 128]
                                if side == 0:
                                    tas[k][a, b, at, q] = tile
                                else:
                                    tbs[k][b, a, at, q] = tile

                if last == end:
                    for d in (2, 1, 3):
                        if side == 0:
                            push(tas[k].at[d], ras[k].at[d - 1], p1_s.at[k, 0], p1_r.at[k, 0], xdev(d))
                        else:
                            push(tbs[k].at[(y + d) % NY], rbs[k].at[d - 1], p1_s.at[k, 1], p1_r.at[k, 1], ydev(d))

    drain(tok.at[0:128], core_r.at[0])
    drain(cot.at[0:128], core_r.at[1])
    drain(w.at[GATE, 0:48, 0:3072], own_yr.at[GATE])
    drain(w.at[UP, 0:48, 0:3072], own_yr.at[UP])
    drain(w.at[DOWN, 0:48], own_xr.at[DOWN])
    forward(0, lambda p: None)
    terms(0)

    o2_bytes = [w.at[DOWN, 0:48], w.at[UP, 0:48, 0:2048], w.at[GATE, 0:64, 0:3072], w.at[UP, 0:64, 0:1536]]
    forward(1, lambda p: drain(o2_bytes[p], o2_r.at[p]))
    terms(1)
    terms(2)

    def both(tokens_at):
        parts = [
            jnp.concatenate([act[0, j, :, tokens_at], act[1, j, :, tokens_at]], axis=0).astype(F32).T
            for j in (2, 1)
        ]
        return jnp.concatenate(parts, axis=1).astype(BF16)

    theirs = both(slice(128, 256))

    @pl.loop(0, 8)
    def _(q):
        cols = pl.ds(pl.multiple_of(q * 512, 512), 512)
        rhs = w[GATE:UP + 1, :, cols].reshape(256, 512)
        ig_send[:, cols] = jnp.dot(theirs, rhs, preferred_element_type=F32).astype(BF16)

    push(ig_send, ig_recv, core_s.at[2], core_r.at[2], partner)

    def input_gradient():
        mine = both(slice(0, 128))
        drain(ig_recv, core_r.at[2])

        @pl.loop(0, 8)
        def _(q):
            cols = pl.ds(pl.multiple_of(q * 512, 512), 512)
            rhs = w[GATE:UP + 1, :, cols].reshape(256, 512)
            total = jnp.dot(mine, rhs, preferred_element_type=F32) + ig_recv[:, cols].astype(F32)
            ig_own[:, cols] = total.astype(BF16)

        pltpu.make_async_copy(ig_own, ig_out, load_sem.at[5]).start()

    def plane_sum(own, got):
        return ((own.astype(F32) + got[0].astype(F32)) + (got[1].astype(F32) + got[2].astype(F32))).astype(BF16)

    def first(k):
        ta, tb, ra, rb, ua, ub, va, vb = (b[k] for b in (tas, tbs, ras, rbs, uas, ubs, vas, vbs))
        drain(ra, p1_r.at[k, 0])
        for d in (2, 1, 3, 0):
            to = (y + d) % NY
            ua[to] = plane_sum(ta[0, to], ra[:, to])
            if d:
                push(ua.at[to], va.at[d - 1], p2_s.at[k, 0], p2_r.at[k, 0], ydev(d))
        drain(rb, p1_r.at[k, 1])
        for d in (2, 1, 3, 0):
            ub[d] = plane_sum(tb[y, d], rb[:, d])
            if d:
                push(ub.at[d], vb.at[d - 1], p2_s.at[k, 1], p2_r.at[k, 1], xdev(d))

    def second(k):
        r = CHUNKS[k][0]
        ua, ub, va, vb, zs, zr = (b[k] for b in (uas, ubs, vas, vbs, zss, zrs))
        n = zs.shape[1]
        drain(va, p2_r.at[k, 0])
        for j in range(n):
            zs[0:4, j] = plane_sum(ua[y, j], va[:, j])
        drain(vb, p2_r.at[k, 1])
        for j in range(n):
            zs[4:8, j] = plane_sum(ub[0, j], vb[:, j])
        if r == 0:
            zr[zl] = zs[zl]
        base = (zh if r == 0 else 1 - zh) * ZLO
        for d in ((4, 3, 5, 2, 6, 1, 7) if r == 0 else range(ZLO)):
            to = (zl + d) % ZLO
            push(zs.at[to], zr.at[zl], z_s.at[k], z_r.at[k], zdev(base + to))

    pl.semaphore_wait(reach, 2)
    first(0)
    first(1)
    input_gradient()
    first(2)
    second(0)
    second(1)
    second(2)
    for k, (r, _, _) in enumerate(CHUNKS):
        drain(zrs[k].at[0:7 + r], z_r.at[k])
    for j in range(3):
        late = zrs[1][:, 0] if j == 0 else zrs[2][:, j - 1]
        grad_out[j] = (jnp.sum(zrs[0][:, j].astype(F32), axis=0) + jnp.sum(late.astype(F32), axis=0)) * scale

    pltpu.make_async_copy(ig_own, ig_out, load_sem.at[5]).wait()
    drain(tok.at[0:128], core_s.at[0])
    drain(cot.at[0:128], core_s.at[1])
    drain(ig_send, core_s.at[2])
    for t in (GATE, UP):
        drain(w.at[t, 0:48, 0:1024], own_xs.at[t])
        drain(w.at[t, 0:48, 0:3072], own_ys.at[t])
    drain(w.at[DOWN, 0:48], own_xs.at[DOWN])

    @pl.when(at_edge)
    def _():
        for p, (t, _, n, _) in enumerate(pieces):
            drain(w.at[t, 0:64, 0:n], hz_s.at[p])

    for p, (t, _, n, _) in enumerate(pieces):
        drain(w.at[t, 0:48, 0:n], o1_s.at[p])
        drain(o2_bytes[p], o2_s.at[p])
    for k, (r, _, _) in enumerate(CHUNKS):
        drain(ras[k], p1_s.at[k, 0])
        drain(rbs[k], p1_s.at[k, 1])
        drain(vas[k], p2_s.at[k, 0])
        drain(vbs[k], p2_s.at[k, 1])
        drain(zss[k].at[0:7 + r], z_s.at[k])


def finish_kernel(ig, grads, ig_out, gate_out, up_out, down_out, sem):
    pairs = [(ig.at[pl.ds(32 * i, 32)], ig_out.at[pl.ds(32 * i, 32)]) for i in range(4)]
    pairs += [(grads.at[2], gate_out), (grads.at[1], up_out), (grads.at[0], down_out)]
    copies = [pltpu.make_async_copy(src, dst, sem.at[i]) for i, (src, dst) in enumerate(pairs)]
    for cp in copies:
        cp.start()
    for cp in copies:
        cp.wait()


def per_device(tokens, cotangent, gate_weight, up_weight, down_weight):
    token_total = tokens.shape[0] * lax.axis_size("dp") * lax.axis_size("pipe")
    scale = float(token_total) ** (-0.5)
    anywhere = pl.BlockSpec(memory_space=pl.ANY)
    inside = pl.BlockSpec(memory_space=pltpu.VMEM)
    share = jax.ShapeDtypeStruct((16, 128), F32)

    def body(*refs):
        panel_kernel(scale, *refs)

    def held(*shape):
        return pltpu.VMEM(shape, BF16)

    def sems(*shape):
        return pltpu.SemaphoreType.DMA(shape)

    def chunked(*dims):
        shapes = [[last - first if d is None else d for d in dims] for _, first, last in CHUNKS]
        return [held(*dims_, 16, 128) for dims_ in shapes]

    ig, grads = pl.pallas_call(
        body,
        out_shape=(jax.ShapeDtypeStruct(tokens.shape, BF16), jax.ShapeDtypeStruct((3, 16, 128), F32)),
        in_specs=[anywhere] * 5,
        out_specs=(anywhere, inside),
        scratch_shapes=[
            held(256, 4096), held(256, 4096), held(3, 128, 4096), held(2, 3, 64, 256),
            held(128, 4096), held(128, 4096), held(128, 4096),
            sems(6), sems(3), sems(3), sems(3), sems(3), sems(2), sems(2), sems(4), sems(4),
            sems(4), sems(4), sems(4), sems(4),
            sems(3, 2), sems(3, 2), sems(3, 2), sems(3, 2), sems(3), sems(3), pltpu.SemaphoreType.REGULAR,
            *chunked(4, 4, None, 4), *chunked(4, 4, None, 4), *chunked(3, 4, None, 4), *chunked(3, 4, None, 4),
            *chunked(4, None, 4), *chunked(4, None, 4), *chunked(3, None, 4), *chunked(3, None, 4),
            *chunked(8, None), *chunked(8, None),
        ],
        compiler_params=pltpu.CompilerParams(
            collective_id=0, has_side_effects=True, vmem_limit_bytes=60 * 2**20
        ),
    )(tokens, cotangent, gate_weight, up_weight, down_weight)
    return pl.pallas_call(
        finish_kernel,
        out_shape=(jax.ShapeDtypeStruct(tokens.shape, BF16), share, share, share),
        in_specs=[inside] * 2,
        out_specs=[anywhere] * 4,
        scratch_shapes=[sems(7)],
    )(ig, grads)


def solution(mesh):
    in_specs = (
        P(("dp", "pipe"), None),
        P(("dp", "pipe"), None),
        P("pipe", None),
        P("pipe", None),
        P("pipe", None),
    )
    out_specs = (P(("dp", "pipe"), None), P("pipe", "dp"), P("pipe", "dp"), P("pipe", "dp"))
    return jax.shard_map(
        per_device, mesh=mesh, in_specs=in_specs, out_specs=out_specs, check_vma=False
    )
```
